32 devices in a mesh: row: 8 (over y, x, core), col: 4 (over z).
Axes of the slice: x: 2, y: 2, z: 4, core: 2. Of those that a mesh axis runs over, the one named last changes fastest.
Arguments:
- a_tiles: bfloat16 [8, 4, 4, 27, 128, 128], P('row', 'col'), as said below
- pattern: int32 [8, 4, 4, 27], P('row', 'col'), may hold values from 0 to 1, as said below
- t_tiles: bfloat16 [8, 4, 4, 128, 128], P('row', 'col'), may hold values from -6 to 6
- colour: int32 [8, 4, 4], replicated, may hold values from 0 to 7, as said below
Outputs:
- prolongator: bfloat16 [8, 4, 4, 8, 128, 128], P('row', 'col')
- restriction_t: bfloat16 [8, 4, 4, 8, 128, 128], P('row', 'col')
The draws below stay inside these ranges and needn't reach their ends.
Inputs may be any that keep to these rules, and one draw needn't show every extreme that they name: pattern[x, y, z, 13] is 1; pattern[x, y, z, o] is 0 where block (x, y - dy, z) or block (x + dx, y, z + dz) lies outside the grid. colour[x, y, z] = 4 p(x) + 2 q(y) + r(z) with p, q, r each 0 or 1. `a_tiles`: the diagonal of every tile with o = 13 is 3.4 or more.
All inputs are finite; a program needn't handle non-finite values.
Results may differ from the reference program's by a relative error of at most 0.0065.
Values may be sent and summed in bfloat16 or wider, within the bound.
A program may use at most 64 MiB of HBM per device.

```python
import jax
import jax.numpy as jnp
from jax import lax

BLK = 128
OFFSETS = 27
SLOTS = 8
GZ = 4
GX = 8
GY = 4


def cut_parity(key, length):
    extents = jax.random.randint(key, (length,), 2, 4)
    cut_ends = jnp.cumsum(extents)
    positions = jnp.arange(length, dtype=jnp.int32)
    aggregate = jnp.sum((cut_ends[None, :] <= positions[:, None]).astype(jnp.int32), axis=1)
    return aggregate % 2


def draw_colour(key, part):
    key = jax.random.fold_in(key, 5)
    x_key, y_key, z_key = jax.random.split(key, 3)
    x_parity = cut_parity(x_key, GX)
    y_parity = cut_parity(y_key, GY)
    z_parity = cut_parity(z_key, GZ)
    return (x_parity[:, None, None] * 4 + y_parity[None, :, None] * 2 + z_parity[None, None, :]).astype(jnp.int32)


def draw_pattern(key, part):
    key = jax.random.fold_in(key, 7)
    level_key, kept_key = jax.random.split(key)
    keep_level = jax.random.randint(level_key, (GX, 1, 1, 1), 3, 11)
    kept = jax.random.randint(kept_key, (GX, GY, GZ, OFFSETS), 0, 10) < keep_level
    offset = jnp.arange(OFFSETS, dtype=jnp.int32)
    x_step = offset // 9 - 1
    y_step = offset // 3 % 3 - 1
    z_step = offset % 3 - 1
    x_place = jnp.arange(GX, dtype=jnp.int32)[:, None, None, None]
    y_place = jnp.arange(GY, dtype=jnp.int32)[None, :, None, None]
    z_place = jnp.arange(GZ, dtype=jnp.int32)[None, None, :, None]
    inside = (y_place - y_step >= 0) & (y_place - y_step < GY)
    inside = inside & (x_place + x_step >= 0) & (x_place + x_step < GX)
    inside = inside & (z_place + z_step >= 0) & (z_place + z_step < GZ)
    return (inside & (kept | (offset == 13))).astype(jnp.int32)


def draw_a_tiles(key, part):
    key = jax.random.fold_in(key, 11)
    entry_key, diagonal_key = jax.random.split(key)
    full_shape = (GX, GY, GZ, OFFSETS, BLK, BLK)
    entries = 0.1 * jax.random.truncated_normal(entry_key, -6.0, 6.0, full_shape, jnp.float32)
    diagonal = jax.random.uniform(diagonal_key, (GX, GY, GZ, 1, BLK, 1), jnp.float32, 4.0, 8.0)
    identity = jnp.eye(BLK, dtype=jnp.float32)
    centre = (jnp.arange(OFFSETS) == 13).astype(jnp.float32)[:, None, None]
    return (entries + diagonal * identity * centre).astype(jnp.bfloat16)


def levels(stream_key, shape, cuts, least, top_value):
    def one(position, shards_of):
        heights = jax.random.uniform(jax.random.fold_in(jax.random.fold_in(stream_key, 6), position), (shards_of,), jnp.float32, least / len(cuts), top_value / len(cuts))
        return jnp.repeat(jnp.exp(heights), shape[position] // shards_of).reshape((-1,) + (1,) * (len(shape) - position - 1))

    factor_of = one(*cuts[0])
    for cut in cuts[1:]:
        factor_of = factor_of * one(*cut)
    return factor_of


def bell_draw(stream_key, extent, deviation, limit, shards=(), kind=jnp.bfloat16):
    values = jax.random.normal(stream_key, extent, jnp.float32) * deviation
    if len(shards) > 0:
        values = levels(stream_key, extent, shards, -0.22, 0.18) * values
    return jnp.clip(values, min=-limit, max=limit).astype(kind)


def setup_inputs(seed: int = 0) -> dict:
    seeds = jax.random.split(jax.random.key(seed), 5)
    a_tiles = draw_a_tiles(jax.random.fold_in(seeds[4], 71), 0)
    pattern = draw_pattern(jax.random.fold_in(seeds[4], 71), 0)
    t_tiles = bell_draw(seeds[2], (GX, GY, GZ, BLK, BLK), 1.0, 6.0, ((0, 8), (1, 4)))
    colour = draw_colour(jax.random.fold_in(seeds[4], 71), 0)
    return {"a_tiles": a_tiles, "pattern": pattern, "t_tiles": t_tiles, "colour": colour}


OMEGA = 2.0 / 3.0
HIGHEST_PRECISION = lax.Precision.HIGHEST


def colour_hot(values):
    return (values[..., None] == jnp.arange(SLOTS, dtype=jnp.int32)).astype(jnp.float32)


def reference(a_tiles, pattern, t_tiles, colour):
    t_pad = jnp.pad(t_tiles, ((1, 1), (1, 1), (1, 1), (0, 0), (0, 0)))
    c_pad = jnp.pad(colour, 1)
    plane_ids = jnp.arange(GX, dtype=jnp.int32)

    def inverse_diagonal(plane):
        coupling = lax.dynamic_index_in_dim(a_tiles, plane, 0, keepdims=False)
        centre = coupling[:, :, 13].astype(jnp.float32)
        return 1.0 / jnp.diagonal(centre, axis1=-2, axis2=-1)

    def own_term(plane):
        selector = colour_hot(lax.dynamic_index_in_dim(colour, plane, 0, keepdims=False))
        tentative = lax.dynamic_index_in_dim(t_tiles, plane, 0, keepdims=False).astype(jnp.float32)
        return selector[..., None, None] * tentative[:, :, None]

    def direct_plane(plane):
        coupling = lax.dynamic_index_in_dim(a_tiles, plane, 0, keepdims=False)
        present = lax.dynamic_index_in_dim(pattern, plane, 0, keepdims=False).astype(jnp.float32)
        t_slab = lax.dynamic_slice_in_dim(t_pad, plane, 3, 0)
        c_slab = lax.dynamic_slice_in_dim(c_pad, plane, 3, 0)
        accumulated = jnp.zeros((GY + 2, GZ, SLOTS, BLK, BLK), jnp.float32)
        for y_step in (-1, 0, 1):
            products, selectors = [], []
            for x_step in (-1, 0, 1):
                for z_step in (-1, 0, 1):
                    offset = (x_step + 1) * 9 + (y_step + 1) * 3 + z_step + 1
                    single = coupling[:, :, offset].astype(jnp.float32) * present[:, :, offset, None, None]
                    partner = t_slab[x_step + 1, 1:GY + 1, 1 + z_step:1 + z_step + GZ].astype(jnp.float32)
                    products.append(jnp.einsum("yzij,yzjm->yzim", single, partner, precision=HIGHEST_PRECISION))
                    selectors.append(colour_hot(c_slab[x_step + 1, 1:GY + 1, 1 + z_step:1 + z_step + GZ]))
            summed = jnp.einsum("oyzs,oyzim->yzsim", jnp.stack(selectors), jnp.stack(products), precision=HIGHEST_PRECISION)
            accumulated = accumulated.at[1 - y_step:1 - y_step + GY].add(summed)
        direct = accumulated[1:GY + 1]
        scale = inverse_diagonal(plane)[:, :, None, :, None]
        return (own_term(plane) - OMEGA * scale * direct).astype(jnp.bfloat16)

    def transposed_plane(plane):
        accumulated = jnp.zeros((GY, GZ + 2, SLOTS, BLK, BLK), jnp.float32)
        for x_step in (-1, 0, 1):
            source = plane - x_step
            inside = ((source >= 0) & (source < GX)).astype(jnp.float32)
            clipped = jnp.clip(source, 0, GX - 1).astype(jnp.int32)
            coupling = lax.dynamic_index_in_dim(a_tiles, clipped, 0, keepdims=False)
            present = lax.dynamic_index_in_dim(pattern, clipped, 0, keepdims=False).astype(jnp.float32) * inside
            t_plane = lax.dynamic_index_in_dim(t_pad, clipped + 1, 0, keepdims=False)
            c_plane = lax.dynamic_index_in_dim(c_pad, clipped + 1, 0, keepdims=False)
            for z_step in (-1, 0, 1):
                products, selectors = [], []
                for y_step in (-1, 0, 1):
                    offset = (x_step + 1) * 9 + (y_step + 1) * 3 + z_step + 1
                    single = coupling[:, :, offset].astype(jnp.float32) * present[:, :, offset, None, None]
                    partner = t_plane[1 - y_step:1 - y_step + GY, 1:GZ + 1].astype(jnp.float32)
                    products.append(jnp.einsum("yzji,yzjm->yzim", single, partner, precision=HIGHEST_PRECISION))
                    selectors.append(colour_hot(c_plane[1 - y_step:1 - y_step + GY, 1:GZ + 1]))
                summed = jnp.einsum("oyzs,oyzim->yzsim", jnp.stack(selectors), jnp.stack(products), precision=HIGHEST_PRECISION)
                accumulated = accumulated.at[:, 1 + z_step:1 + z_step + GZ].add(summed)
        transposed = accumulated[:, 1:GZ + 1]
        scale = inverse_diagonal(plane)[:, :, None, :, None]
        return (own_term(plane) - OMEGA * scale * transposed).astype(jnp.bfloat16)

    prolongator = lax.map(direct_plane, plane_ids)
    restriction_t = lax.map(transposed_plane, plane_ids)
    return prolongator, restriction_t
```

```python
import functools

import jax
import jax.numpy as jnp
from jax import lax
from jax.experimental import pallas as pl
from jax.experimental.pallas import tpu as pltpu
from jax.sharding import PartitionSpec as P

SLOTS = 8
OMEGA = 2.0 / 3.0
BF = jnp.bfloat16
F32 = jnp.float32


def kernel(
    nx, ny, nz, blk,
    pattern, colour, a_hbm, t_own, pro_hbm, res_hbm,
    a_v, th, td, tt, sbuf, rbuf, own, obuf,
    a_sem, th_send, th_recv, p_send, p_recv, o_sem,
):
    x = lax.axis_index("row")
    y = lax.axis_index("col")
    has_dst = (x > 0, x < nx - 1, y > 0, y < ny - 1)
    has_src = (x < nx - 1, x > 0, y < ny - 1, y > 0)
    peers = ((x - 1, y), (x + 1, y), (x, y - 1), (x, y + 1))

    def a_copy(z):
        return pltpu.make_async_copy(a_hbm.at[0, 0, z], a_v.at[z], a_sem.at[z])

    for z in range(nz):
        a_copy(z).start()

    barrier = pltpu.get_barrier_semaphore()
    for d in range(4):
        @pl.when(has_dst[d])
        def _():
            pl.semaphore_signal(
                barrier, inc=1, device_id=peers[d], device_id_type=pl.DeviceIdType.MESH
            )
    count = sum(h.astype(jnp.int32) for h in has_dst)
    pl.semaphore_wait(barrier, count)

    def t_copy(d):
        return pltpu.make_async_remote_copy(
            src_ref=t_own.at[0, 0], dst_ref=th.at[d],
            send_sem=th_send.at[d], recv_sem=th_recv.at[d],
            device_id=peers[d], device_id_type=pl.DeviceIdType.MESH,
        )

    def p_copy(d, z):
        return pltpu.make_async_remote_copy(
            src_ref=sbuf.at[d, z], dst_ref=rbuf.at[d, z],
            send_sem=p_send.at[d, z], recv_sem=p_recv.at[d, z],
            device_id=peers[d], device_id_type=pl.DeviceIdType.MESH,
        )

    for d in (2, 3, 0, 1):
        @pl.when(has_dst[d])
        def _():
            t_copy(d).start()

    for d in range(4):
        @pl.when(jnp.logical_not(has_src[d]))
        def _():
            th[d] = jnp.zeros(th.shape[1:], BF)
            rbuf[d] = jnp.zeros(rbuf.shape[1:], BF)

    def bit(value, shift):
        return ((value >> shift) & 1).astype(F32)

    def p_of(i):
        return bit(colour[jnp.clip(i, 0, nx - 1), 0, 0], 2)

    def q_of(j):
        return bit(colour[0, jnp.clip(j, 0, ny - 1), 0], 1)

    def r_of(z):
        return bit(colour[0, 0, z], 0)

    def hits(value):
        return (1.0 - value, value)

    def times(tile, scalar):
        return tile * jnp.full(tile.shape, scalar, F32).astype(BF)

    def place(dst, which, high, source):
        zero = jnp.zeros((blk, 4 * blk), BF)
        dst[which, 0:blk, :] = zero
        dst[which, (nz + 1) * blk : (nz + 2) * blk, :] = zero

        def step(z, carry):
            tile = source(z)
            rows = pl.ds(pl.multiple_of((z + 1) * blk, blk), blk)
            r = r_of(z)
            for h in range(2):
                for l in range(2):
                    dst[which, rows, pl.ds((2 * h + l) * blk, blk)] = times(
                        tile, hits(high)[h] * hits(r)[l]
                    )
            return carry

        lax.fori_loop(0, nz, step, 0)

    place(td, 1, p_of(x), lambda z: t_own[0, 0, z])
    place(tt, 1, q_of(y), lambda z: t_own[0, 0, z])

    def mask_step(z, carry):
        a_copy(z).wait()
        for o in range(27):
            a_v[z, o] = times(a_v[z, o], pattern[0, 0, z, o].astype(F32))
        return carry

    lax.fori_loop(0, nz, mask_step, 0)

    for d, dst, which, high in (
        (0, td, 2, p_of(x + 1)),
        (1, td, 0, p_of(x - 1)),
        (2, tt, 2, q_of(y + 1)),
        (3, tt, 0, q_of(y - 1)),
    ):
        @pl.when(has_src[d])
        def _():
            t_copy(d).wait_recv()
        place(dst, which, high, lambda z, d=d: th[d, z])

    def direct(z, y_steps):
        rows = pl.ds(pl.multiple_of(z * blk, blk), 3 * blk)
        right = jnp.concatenate([td[i, rows, :] for i in range(3)], axis=0)
        left = jnp.concatenate(
            [
                jnp.concatenate(
                    [a_v[z, i * 9 + (dy + 1) * 3 + k] for i in range(3) for k in range(3)], axis=1
                )
                for dy in y_steps
            ],
            axis=0,
        )
        return jnp.dot(left, right, preferred_element_type=F32)

    def transposed(z, x_steps):
        rows = pl.ds(pl.multiple_of(z * blk, blk), 3 * blk)
        right = jnp.concatenate([tt[j, rows, :] for j in range(3)], axis=0)
        left = jnp.concatenate(
            [
                jnp.concatenate(
                    [
                        a_v[jnp.clip(z - 1 + e, 0, nz - 1), (dx + 1) * 9 + (2 - j) * 3 + 2 - e]
                        for dx in x_steps
                    ],
                    axis=1,
                )
                for j in range(3)
                for e in range(3)
            ],
            axis=0,
        )
        return lax.dot_general(
            left, right, (((0,), (0,)), ((), ())), preferred_element_type=F32
        )

    def edge_step(z, carry):
        part = direct(z, (1, -1)).astype(BF)
        sbuf[2, z] = part[:blk]
        sbuf[3, z] = part[blk:]
        for d in (2, 3):
            @pl.when(has_dst[d])
            def _():
                p_copy(d, z).start()
        part = transposed(z, (-1, 1)).astype(BF)
        sbuf[0, z] = part[:blk]
        sbuf[1, z] = part[blk:]
        for d in (0, 1):
            @pl.when(has_dst[d])
            def _():
                p_copy(d, z).start()
        return carry

    lax.fori_loop(0, nz, edge_step, 0)

    def own_step(z, carry):
        own[0, z] = direct(z, (0,))
        own[1, z] = transposed(z, (0,))
        return carry

    lax.fori_loop(0, nz, own_step, 0)

    px, qy = p_of(x), q_of(y)
    diagonal = lax.broadcasted_iota(jnp.int32, (blk, blk), 0) == lax.broadcasted_iota(
        jnp.int32, (blk, blk), 1
    )

    def out_copy(which, z):
        out = (pro_hbm, res_hbm)[which]
        return pltpu.make_async_copy(obuf.at[which, z], out.at[0, 0, z], o_sem.at[which, z])

    def final_step(z, carry):
        centre = jnp.where(diagonal, a_v[z, 13].astype(F32), 0.0)
        scale = OMEGA / jnp.sum(centre, axis=1, keepdims=True)
        tile = t_own[0, 0, z].astype(F32)
        r = r_of(z)
        for which in (1, 0):
            first = 2 if which == 0 else 0
            for d in (first, first + 1):
                @pl.when(has_src[d])
                def _():
                    p_copy(d, z).wait_recv()
            here, above, below = (
                (qy, q_of(y + 1), q_of(y - 1)) if which == 0 else (px, p_of(x + 1), p_of(x - 1))
            )
            for h in range(2):
                for l in range(2):
                    columns = pl.ds((2 * h + l) * blk, blk)
                    mine = own[which, z, :, columns] * scale
                    up = rbuf[first, z, :, columns].astype(F32) * scale
                    down = rbuf[first + 1, z, :, columns].astype(F32) * scale
                    for v in range(2):
                        total = (
                            mine * hits(here)[v] + up * hits(above)[v] + down * hits(below)[v]
                        )
                        p, q = (h, v) if which == 0 else (v, h)
                        keep = hits(px)[p] * hits(qy)[q] * hits(r)[l]
                        obuf[which, z, 4 * p + 2 * q + l] = (tile * keep - total).astype(BF)
            out_copy(which, z).start()
        return carry

    lax.fori_loop(0, nz, final_step, 0)

    for z in range(nz):
        out_copy(0, z).wait()
        out_copy(1, z).wait()
        for d in range(4):
            @pl.when(has_dst[d])
            def _():
                p_copy(d, z).wait_send()
    for d in range(4):
        @pl.when(has_dst[d])
        def _():
            t_copy(d).wait_send()


def body(nx, ny, a_tiles, pattern, t_tiles, colour):
    nz, blk = a_tiles.shape[2], a_tiles.shape[-1]
    out = jax.ShapeDtypeStruct((1, 1, nz, SLOTS, blk, blk), BF)
    return pl.pallas_call(
        functools.partial(kernel, nx, ny, nz, blk),
        out_shape=(out, out),
        in_specs=[
            pl.BlockSpec(memory_space=pltpu.SMEM),
            pl.BlockSpec(memory_space=pltpu.SMEM),
            pl.BlockSpec(memory_space=pl.ANY),
            pl.BlockSpec(memory_space=pltpu.VMEM),
        ],
        out_specs=(pl.BlockSpec(memory_space=pl.ANY),) * 2,
        scratch_shapes=[
            pltpu.VMEM((nz, 27, blk, blk), BF),
            pltpu.VMEM((4, nz, blk, blk), BF),
            pltpu.VMEM((3, (nz + 2) * blk, 4 * blk), BF),
            pltpu.VMEM((3, (nz + 2) * blk, 4 * blk), BF),
            pltpu.VMEM((4, nz, blk, 4 * blk), BF),
            pltpu.VMEM((4, nz, blk, 4 * blk), BF),
            pltpu.VMEM((2, nz, blk, 4 * blk), F32),
            pltpu.VMEM((2, nz, SLOTS, blk, blk), BF),
            pltpu.SemaphoreType.DMA((nz,)),
            pltpu.SemaphoreType.DMA((4,)),
            pltpu.SemaphoreType.DMA((4,)),
            pltpu.SemaphoreType.DMA((4, nz)),
            pltpu.SemaphoreType.DMA((4, nz)),
            pltpu.SemaphoreType.DMA((2, nz)),
        ],
        compiler_params=pltpu.CompilerParams(
            collective_id=0, has_side_effects=True, vmem_limit_bytes=48 * 1024 * 1024
        ),
        cost_estimate=pl.CostEstimate(
            flops=3_600_000_000, bytes_accessed=6_000_000, transcendentals=0
        ),
    )(pattern, colour, a_tiles, t_tiles)


def solution(mesh):
    in_specs = (
        P("row", "col", None, None, None, None),
        P("row", "col", None, None),
        P("row", "col", None, None, None),
        P(),
    )
    out_specs = (P("row", "col", None, None, None, None), P("row", "col", None, None, None, None))
    fn = functools.partial(body, mesh.shape["row"], mesh.shape["col"])
    return jax.shard_map(fn, mesh=mesh, in_specs=in_specs, out_specs=out_specs, check_vma=False)
```

```python
import functools

import jax
import jax.numpy as jnp
from jax import lax
from jax.experimental import pallas as pl
from jax.experimental.pallas import tpu as pltpu
from jax.sharding import PartitionSpec as P

SLOTS = 8
OMEGA = 2.0 / 3.0
BF = jnp.bfloat16
F32 = jnp.float32


def kernel(
    nx, ny, nz, blk,
    pattern_hbm, colour_hbm, a_hbm, t_hbm, pro, res,
    pattern, colour, t_own, a_v, th, td, tt, sbuf, rbuf, own,
    in_sem, a_sem, th_send, th_recv, p_send, p_recv,
):
    x = lax.axis_index("row")
    y = lax.axis_index("col")
    has_dst = (x > 0, x < nx - 1, y > 0, y < ny - 1)
    has_src = (x < nx - 1, x > 0, y < ny - 1, y > 0)
    peers = ((x - 1, y), (x + 1, y), (x, y - 1), (x, y + 1))

    def a_copy(z):
        return pltpu.make_async_copy(a_hbm.at[0, 0, z], a_v.at[z], a_sem.at[z])

    t_in = pltpu.make_async_copy(t_hbm, t_own, in_sem.at[0])
    colour_in = pltpu.make_async_copy(colour_hbm, colour, in_sem.at[1])
    pattern_in = pltpu.make_async_copy(pattern_hbm, pattern, in_sem.at[2])
    colour_in.start()
    pattern_in.start()
    t_in.start()
    for z in range(nz):
        a_copy(z).start()

    barrier = pltpu.get_barrier_semaphore()
    for d in range(4):
        @pl.when(has_dst[d])
        def _():
            pl.semaphore_signal(
                barrier, inc=1, device_id=peers[d], device_id_type=pl.DeviceIdType.MESH
            )
    count = sum(h.astype(jnp.int32) for h in has_dst)
    pl.semaphore_wait(barrier, count)

    def t_copy(d):
        return pltpu.make_async_remote_copy(
            src_ref=t_hbm.at[0, 0], dst_ref=th.at[d],
            send_sem=th_send.at[d], recv_sem=th_recv.at[d],
            device_id=peers[d], device_id_type=pl.DeviceIdType.MESH,
        )

    def p_copy(d, z):
        return pltpu.make_async_remote_copy(
            src_ref=sbuf.at[d, z], dst_ref=rbuf.at[d, z],
            send_sem=p_send.at[d, z], recv_sem=p_recv.at[d, z],
            device_id=peers[d], device_id_type=pl.DeviceIdType.MESH,
        )

    for d in (2, 3, 0, 1):
        @pl.when(has_dst[d])
        def _():
            t_copy(d).start()

    for d in range(4):
        @pl.when(jnp.logical_not(has_src[d]))
        def _():
            th[d] = jnp.zeros(th.shape[1:], BF)
            rbuf[d] = jnp.zeros(rbuf.shape[1:], BF)

    def bit(value, shift):
        return ((value >> shift) & 1).astype(F32)

    def p_of(i):
        return bit(colour[0, 0, jnp.clip(i, 0, nx - 1)], 2)

    def q_of(j):
        return bit(colour[jnp.clip(j, 0, ny - 1), 0, 0], 1)

    def r_of(z):
        return bit(colour[0, z, 0], 0)

    def hits(value):
        return (1.0 - value, value)

    def times(tile, scalar):
        return tile * jnp.full(tile.shape, scalar, F32).astype(BF)

    def place(dst, which, high, source):
        zero = jnp.zeros((blk, 4 * blk), BF)
        dst[which, 0:blk, :] = zero
        dst[which, (nz + 1) * blk : (nz + 2) * blk, :] = zero

        def step(z, carry):
            tile = source(z)
            rows = pl.ds(pl.multiple_of((z + 1) * blk, blk), blk)
            r = r_of(z)
            for h in range(2):
                for l in range(2):
                    dst[which, rows, pl.ds((2 * h + l) * blk, blk)] = times(
                        tile, hits(high)[h] * hits(r)[l]
                    )
            return carry

        lax.fori_loop(0, nz, step, 0)

    colour_in.wait()
    t_in.wait()
    place(td, 1, p_of(x), lambda z: t_own[0, 0, z])
    place(tt, 1, q_of(y), lambda z: t_own[0, 0, z])

    pattern_in.wait()

    def mask_step(z, carry):
        a_copy(z).wait()
        for o in range(27):
            a_v[z, o] = times(a_v[z, o], pattern[0, 0, z, o].astype(F32))
        return carry

    lax.fori_loop(0, nz, mask_step, 0)

    for d, dst, which, high in (
        (0, td, 2, p_of(x + 1)),
        (1, td, 0, p_of(x - 1)),
        (2, tt, 2, q_of(y + 1)),
        (3, tt, 0, q_of(y - 1)),
    ):
        @pl.when(has_src[d])
        def _():
            t_copy(d).wait_recv()
        place(dst, which, high, lambda z, d=d: th[d, z])

    def direct(z, y_steps):
        rows = pl.ds(pl.multiple_of(z * blk, blk), 3 * blk)
        right = jnp.concatenate([td[i, rows, :] for i in range(3)], axis=0)
        left = jnp.concatenate(
            [
                jnp.concatenate(
                    [a_v[z, i * 9 + (dy + 1) * 3 + k] for i in range(3) for k in range(3)], axis=1
                )
                for dy in y_steps
            ],
            axis=0,
        )
        return jnp.dot(left, right, preferred_element_type=F32)

    def transposed(z, x_steps):
        rows = pl.ds(pl.multiple_of(z * blk, blk), 3 * blk)
        right = jnp.concatenate([tt[j, rows, :] for j in range(3)], axis=0)
        left = jnp.concatenate(
            [
                jnp.concatenate(
                    [
                        a_v[jnp.clip(z - 1 + e, 0, nz - 1), (dx + 1) * 9 + (2 - j) * 3 + 2 - e]
                        for dx in x_steps
                    ],
                    axis=1,
                )
                for j in range(3)
                for e in range(3)
            ],
            axis=0,
        )
        return lax.dot_general(
            left, right, (((0,), (0,)), ((), ())), preferred_element_type=F32
        )

    def edge_step(z, carry):
        part = direct(z, (1, -1)).astype(BF)
        sbuf[2, z] = part[:blk]
        sbuf[3, z] = part[blk:]
        for d in (2, 3):
            @pl.when(has_dst[d])
            def _():
                p_copy(d, z).start()
        part = transposed(z, (-1, 1)).astype(BF)
        sbuf[0, z] = part[:blk]
        sbuf[1, z] = part[blk:]
        for d in (0, 1):
            @pl.when(has_dst[d])
            def _():
                p_copy(d, z).start()
        return carry

    lax.fori_loop(0, nz, edge_step, 0)

    def own_step(z, carry):
        own[0, z] = direct(z, (0,))
        own[1, z] = transposed(z, (0,))
        return carry

    lax.fori_loop(0, nz, own_step, 0)

    px, qy = p_of(x), q_of(y)
    diagonal = lax.broadcasted_iota(jnp.int32, (blk, blk), 0) == lax.broadcasted_iota(
        jnp.int32, (blk, blk), 1
    )

    def final_step(z, carry):
        centre = jnp.where(diagonal, a_v[z, 13].astype(F32), 0.0)
        scale = OMEGA / jnp.sum(centre, axis=1, keepdims=True)
        tile = t_own[0, 0, z].astype(F32)
        r = r_of(z)
        for which in (1, 0):
            first = 2 if which == 0 else 0
            for d in (first, first + 1):
                @pl.when(has_src[d])
                def _():
                    p_copy(d, z).wait_recv()
            here, above, below = (
                (qy, q_of(y + 1), q_of(y - 1)) if which == 0 else (px, p_of(x + 1), p_of(x - 1))
            )
            for h in range(2):
                for l in range(2):
                    columns = pl.ds((2 * h + l) * blk, blk)
                    mine = own[which, z, :, columns] * scale
                    up = rbuf[first, z, :, columns].astype(F32) * scale
                    down = rbuf[first + 1, z, :, columns].astype(F32) * scale
                    for v in range(2):
                        total = (
                            mine * hits(here)[v] + up * hits(above)[v] + down * hits(below)[v]
                        )
                        p, q = (h, v) if which == 0 else (v, h)
                        keep = hits(px)[p] * hits(qy)[q] * hits(r)[l]
                        (pro, res)[which][0, 0, z, 4 * p + 2 * q + l] = (tile * keep - total).astype(BF)
        return carry

    lax.fori_loop(0, nz, final_step, 0)

    for z in range(nz):
        for d in range(4):
            @pl.when(has_dst[d])
            def _():
                p_copy(d, z).wait_send()
    for d in range(4):
        @pl.when(has_dst[d])
        def _():
            t_copy(d).wait_send()


def store_kernel(pro, res, pro_hbm, res_hbm, sem):
    nz = pro.shape[2]
    copies = [
        pltpu.make_async_copy(src.at[0, 0, z], dst.at[0, 0, z], sem.at[i, z])
        for i, (src, dst) in enumerate(((pro, pro_hbm), (res, res_hbm)))
        for z in range(nz)
    ]
    for copy in copies:
        copy.start()
    for copy in copies:
        copy.wait()


def body(nx, ny, a_tiles, pattern, t_tiles, colour):
    nz, blk = a_tiles.shape[2], a_tiles.shape[-1]
    colour = jnp.transpose(colour, (1, 2, 0))
    out = jax.ShapeDtypeStruct((1, 1, nz, SLOTS, blk, blk), BF)
    hbm = pl.BlockSpec(memory_space=pltpu.HBM)
    vmem = pl.BlockSpec(memory_space=pltpu.VMEM)
    pro, res = pl.pallas_call(
        functools.partial(kernel, nx, ny, nz, blk),
        out_shape=(out, out),
        in_specs=[hbm] * 4,
        out_specs=(vmem, vmem),
        scratch_shapes=[
            pltpu.SMEM(pattern.shape, jnp.int32),
            pltpu.SMEM(colour.shape, jnp.int32),
            pltpu.VMEM(t_tiles.shape, BF),
            pltpu.VMEM((nz, 27, blk, blk), BF),
            pltpu.VMEM((4, nz, blk, blk), BF),
            pltpu.VMEM((3, (nz + 2) * blk, 4 * blk), BF),
            pltpu.VMEM((3, (nz + 2) * blk, 4 * blk), BF),
            pltpu.VMEM((4, nz, blk, 4 * blk), BF),
            pltpu.VMEM((4, nz, blk, 4 * blk), BF),
            pltpu.VMEM((2, nz, blk, 4 * blk), F32),
            pltpu.SemaphoreType.DMA((3,)),
            pltpu.SemaphoreType.DMA((nz,)),
            pltpu.SemaphoreType.DMA((4,)),
            pltpu.SemaphoreType.DMA((4,)),
            pltpu.SemaphoreType.DMA((4, nz)),
            pltpu.SemaphoreType.DMA((4, nz)),
        ],
        compiler_params=pltpu.CompilerParams(
            collective_id=0, has_side_effects=True, vmem_limit_bytes=48 * 1024 * 1024
        ),
        cost_estimate=pl.CostEstimate(
            flops=3_600_000_000, bytes_accessed=6_000_000, transcendentals=0
        ),
    )(*(pltpu.with_memory_space_constraint(v, pltpu.HBM) for v in (pattern, colour, a_tiles, t_tiles)))
    return pl.pallas_call(
        store_kernel,
        out_shape=(out, out),
        in_specs=[vmem, vmem],
        out_specs=(hbm, hbm),
        scratch_shapes=[pltpu.SemaphoreType.DMA((2, nz))],
    )(pro, res)


def solution(mesh):
    in_specs = (
        P("row", "col", None, None, None, None),
        P("row", "col", None, None),
        P("row", "col", None, None, None),
        P(),
    )
    out_specs = (P("row", "col", None, None, None, None), P("row", "col", None, None, None, None))
    fn = functools.partial(body, mesh.shape["row"], mesh.shape["col"])
    return jax.shard_map(fn, mesh=mesh, in_specs=in_specs, out_specs=out_specs, check_vma=False)
```

```python
import functools

import jax
import jax.numpy as jnp
from jax import lax
from jax.experimental import pallas as pl
from jax.experimental.pallas import tpu as pltpu
from jax.sharding import PartitionSpec as P

SLOTS = 8
OMEGA = 2.0 / 3.0
BF = jnp.bfloat16
F32 = jnp.float32


def kernel(
    nx, ny, nz, blk,
    pattern_hbm, colour_hbm, a_hbm, t_hbm, pro, res,
    pattern, colour, t_own, a_v, th, td, tt, sbuf, rbuf, own,
    in_sem, a_sem, th_send, th_recv, p_send, p_recv,
):
    x = lax.axis_index("row")
    y = lax.axis_index("col")
    has_dst = (x > 0, x < nx - 1, y > 0, y < ny - 1)
    has_src = (x < nx - 1, x > 0, y < ny - 1, y > 0)
    peers = ((x - 1, y), (x + 1, y), (x, y - 1), (x, y + 1))

    def a_copy(z):
        return pltpu.make_async_copy(a_hbm.at[0, 0, z], a_v.at[z], a_sem.at[z])

    t_in = pltpu.make_async_copy(t_hbm, t_own, in_sem.at[0])
    colour_in = pltpu.make_async_copy(colour_hbm, colour, in_sem.at[1])
    pattern_in = pltpu.make_async_copy(pattern_hbm, pattern, in_sem.at[2])
    colour_in.start()
    pattern_in.start()
    t_in.start()
    for z in range(nz):
        a_copy(z).start()

    barrier = pltpu.get_barrier_semaphore()
    for d in range(4):
        @pl.when(has_dst[d])
        def _():
            pl.semaphore_signal(
                barrier, inc=1, device_id=peers[d], device_id_type=pl.DeviceIdType.MESH
            )
    count = sum(h.astype(jnp.int32) for h in has_dst)
    pl.semaphore_wait(barrier, count)

    def t_copy(d):
        return pltpu.make_async_remote_copy(
            src_ref=t_hbm.at[0, 0], dst_ref=th.at[d],
            send_sem=th_send.at[d], recv_sem=th_recv.at[d],
            device_id=peers[d], device_id_type=pl.DeviceIdType.MESH,
        )

    def p_copy(d, z):
        return pltpu.make_async_remote_copy(
            src_ref=sbuf.at[d, z], dst_ref=rbuf.at[d, z],
            send_sem=p_send.at[d, z], recv_sem=p_recv.at[d, z],
            device_id=peers[d], device_id_type=pl.DeviceIdType.MESH,
        )

    for d in (2, 3, 0, 1):
        @pl.when(has_dst[d])
        def _():
            t_copy(d).start()

    for d in range(4):
        @pl.when(jnp.logical_not(has_src[d]))
        def _():
            th[d] = jnp.zeros(th.shape[1:], BF)
            rbuf[d] = jnp.zeros(rbuf.shape[1:], BF)

    def bit(value, shift):
        return ((value >> shift) & 1).astype(F32)

    def p_of(i):
        return bit(colour[0, 0, jnp.clip(i, 0, nx - 1)], 2)

    def q_of(j):
        return bit(colour[jnp.clip(j, 0, ny - 1), 0, 0], 1)

    def r_of(z):
        return bit(colour[0, z, 0], 0)

    def hits(value):
        return (1.0 - value, value)

    def times(tile, scalar):
        return tile * jnp.full(tile.shape, scalar, F32).astype(BF)

    def place(dst, which, high, source):
        zero = jnp.zeros((blk, 4 * blk), BF)
        dst[which, 0:blk, :] = zero
        dst[which, (nz + 1) * blk : (nz + 2) * blk, :] = zero

        def step(z, carry):
            tile = source(z)
            rows = pl.ds(pl.multiple_of((z + 1) * blk, blk), blk)
            r = r_of(z)
            for h in range(2):
                for l in range(2):
                    dst[which, rows, pl.ds((2 * h + l) * blk, blk)] = times(
                        tile, hits(high)[h] * hits(r)[l]
                    )
            return carry

        lax.fori_loop(0, nz, step, 0)

    colour_in.wait()
    t_in.wait()
    place(td, 1, p_of(x), lambda z: t_own[0, 0, z])
    place(tt, 1, q_of(y), lambda z: t_own[0, 0, z])

    pattern_in.wait()

    def mask_step(z, carry):
        a_copy(z).wait()
        for o in range(27):
            a_v[z, o] = times(a_v[z, o], pattern[0, 0, z, o].astype(F32))
        return carry

    lax.fori_loop(0, nz, mask_step, 0)

    for d, dst, which, high in (
        (0, td, 2, p_of(x + 1)),
        (1, td, 0, p_of(x - 1)),
        (2, tt, 2, q_of(y + 1)),
        (3, tt, 0, q_of(y - 1)),
    ):
        @pl.when(has_src[d])
        def _():
            t_copy(d).wait_recv()
        place(dst, which, high, lambda z, d=d: th[d, z])

    def direct(z, y_steps):
        rows = pl.ds(pl.multiple_of(z * blk, blk), 3 * blk)
        right = jnp.concatenate([td[i, rows, :] for i in range(3)], axis=0)
        left = jnp.concatenate(
            [
                jnp.concatenate(
                    [a_v[z, i * 9 + (dy + 1) * 3 + k] for i in range(3) for k in range(3)], axis=1
                )
                for dy in y_steps
            ],
            axis=0,
        )
        return jnp.dot(left, right, preferred_element_type=F32)

    def transposed(z, x_steps):
        rows = pl.ds(pl.multiple_of(z * blk, blk), 3 * blk)
        right = jnp.concatenate([tt[j, rows, :] for j in range(3)], axis=0)
        left = jnp.concatenate(
            [
                jnp.concatenate(
                    [
                        a_v[jnp.clip(z - 1 + e, 0, nz - 1), (dx + 1) * 9 + (2 - j) * 3 + 2 - e]
                        for dx in x_steps
                    ],
                    axis=1,
                )
                for j in range(3)
                for e in range(3)
            ],
            axis=0,
        )
        return lax.dot_general(
            left, right, (((0,), (0,)), ((), ())), preferred_element_type=F32
        )

    def edge_step(z, carry):
        part = direct(z, (1, -1)).astype(BF)
        sbuf[2, z] = part[:blk]
        sbuf[3, z] = part[blk:]
        for d in (2, 3):
            @pl.when(has_dst[d])
            def _():
                p_copy(d, z).start()
        part = transposed(z, (-1, 1)).astype(BF)
        sbuf[0, z] = part[:blk]
        sbuf[1, z] = part[blk:]
        for d in (0, 1):
            @pl.when(has_dst[d])
            def _():
                p_copy(d, z).start()
        return carry

    lax.fori_loop(0, nz, edge_step, 0)

    def own_step(z, carry):
        own[0, z] = direct(z, (0,))
        own[1, z] = transposed(z, (0,))
        return carry

    lax.fori_loop(0, nz, own_step, 0)

    px, qy = p_of(x), q_of(y)
    diagonal = lax.broadcasted_iota(jnp.int32, (blk, blk), 0) == lax.broadcasted_iota(
        jnp.int32, (blk, blk), 1
    )

    def final_step(z, carry):
        centre = jnp.where(diagonal, a_v[z, 13].astype(F32), 0.0)
        scale = OMEGA / jnp.sum(centre, axis=1, keepdims=True)
        tile = t_own[0, 0, z].astype(F32)
        r = r_of(z)
        for which in (1, 0):
            first = 2 if which == 0 else 0
            for d in (first, first + 1):
                @pl.when(has_src[d])
                def _():
                    p_copy(d, z).wait_recv()
            here, above, below = (
                (qy, q_of(y + 1), q_of(y - 1)) if which == 0 else (px, p_of(x + 1), p_of(x - 1))
            )
            for h in range(2):
                for l in range(2):
                    columns = pl.ds((2 * h + l) * blk, blk)
                    mine = own[which, z, :, columns] * scale
                    up = rbuf[first, z, :, columns].astype(F32) * scale
                    down = rbuf[first + 1, z, :, columns].astype(F32) * scale
                    for v in range(2):
                        total = (
                            mine * hits(here)[v] + up * hits(above)[v] + down * hits(below)[v]
                        )
                        p, q = (h, v) if which == 0 else (v, h)
                        keep = hits(px)[p] * hits(qy)[q] * hits(r)[l]
                        (pro, res)[which][0, 0, z, 4 * p + 2 * q + l] = (tile * keep - total).astype(BF)
        return carry

    lax.fori_loop(0, nz, final_step, 0)

    for z in range(nz):
        for d in range(4):
            @pl.when(has_dst[d])
            def _():
                p_copy(d, z).wait_send()
    for d in range(4):
        @pl.when(has_dst[d])
        def _():
            t_copy(d).wait_send()


def store_kernel(pro, res, pro_hbm, res_hbm, sem):
    nz = pro.shape[2]
    copies = [
        pltpu.make_async_copy(src.at[0, 0, z], dst.at[0, 0, z], sem.at[i, z])
        for i, (src, dst) in enumerate(((pro, pro_hbm), (res, res_hbm)))
        for z in range(nz)
    ]
    for copy in copies:
        copy.start()
    for copy in copies:
        copy.wait()


def body(nx, ny, a_tiles, pattern, t_tiles, colour):
    nz, blk = a_tiles.shape[2], a_tiles.shape[-1]
    colour = jnp.transpose(colour, (1, 2, 0))
    out = jax.ShapeDtypeStruct((1, 1, nz, SLOTS, blk, blk), BF)
    hbm = pl.BlockSpec(memory_space=pltpu.HBM)
    vmem = pl.BlockSpec(memory_space=pltpu.VMEM)
    pro, res = pl.pallas_call(
        functools.partial(kernel, nx, ny, nz, blk),
        out_shape=(out, out),
        in_specs=[hbm] * 4,
        out_specs=(vmem, vmem),
        scratch_shapes=[
            pltpu.SMEM(pattern.shape, jnp.int32),
            pltpu.SMEM(colour.shape, jnp.int32),
            pltpu.VMEM(t_tiles.shape, BF),
            pltpu.VMEM((nz, 27, blk, blk), BF),
            pltpu.VMEM((4, nz, blk, blk), BF),
            pltpu.VMEM((3, (nz + 2) * blk, 4 * blk), BF),
            pltpu.VMEM((3, (nz + 2) * blk, 4 * blk), BF),
            pltpu.VMEM((4, nz, blk, 4 * blk), BF),
            pltpu.VMEM((4, nz, blk, 4 * blk), BF),
            pltpu.VMEM((2, nz, blk, 4 * blk), F32),
            pltpu.SemaphoreType.DMA((3,)),
            pltpu.SemaphoreType.DMA((nz,)),
            pltpu.SemaphoreType.DMA((4,)),
            pltpu.SemaphoreType.DMA((4,)),
            pltpu.SemaphoreType.DMA((4, nz)),
            pltpu.SemaphoreType.DMA((4, nz)),
        ],
        compiler_params=pltpu.CompilerParams(
            collective_id=0, has_side_effects=True, vmem_limit_bytes=28 * 1024 * 1024
        ),
        cost_estimate=pl.CostEstimate(
            flops=3_600_000_000, bytes_accessed=6_000_000, transcendentals=0
        ),
    )(*(pltpu.with_memory_space_constraint(v, pltpu.HBM) for v in (pattern, colour, a_tiles, t_tiles)))
    return pl.pallas_call(
        store_kernel,
        out_shape=(out, out),
        in_specs=[vmem, vmem],
        out_specs=(hbm, hbm),
        scratch_shapes=[pltpu.SemaphoreType.DMA((2, nz))],compiler_params=pltpu.CompilerParams(vmem_limit_bytes=2*1024*1024),
    )(pro, res)


def solution(mesh):
    in_specs = (
        P("row", "col", None, None, None, None),
        P("row", "col", None, None),
        P("row", "col", None, None, None),
        P(),
    )
    out_specs = (P("row", "col", None, None, None, None), P("row", "col", None, None, None, None))
    fn = functools.partial(body, mesh.shape["row"], mesh.shape["col"])
    return jax.shard_map(fn, mesh=mesh, in_specs=in_specs, out_specs=out_specs, check_vma=False)
```

```python
import functools

import jax
import jax.numpy as jnp
from jax import lax
from jax.experimental import pallas as pl
from jax.experimental.pallas import tpu as pltpu
from jax.sharding import PartitionSpec as P

SLOTS = 8
OMEGA = 2.0 / 3.0
BF = jnp.bfloat16
F32 = jnp.float32


def kernel(
    nx, ny, nz, blk,
    pattern_hbm, colour_hbm, a_hbm, t_hbm, pro, res,
    pattern, colour, t_own, a_v, th, td, tt, sbuf, rbuf, own, hop,
    in_sem, a_sem, th_send, th_recv, p_send, p_recv, h_send, h_recv, f_send,
):
    x = lax.axis_index("row")
    y = lax.axis_index("col")
    has_dst = (x > 0, x < nx - 1, y > 0, y < ny - 1)
    has_src = (x < nx - 1, x > 0, y < ny - 1, y > 0)
    peers = ((x - 1, y), (x + 1, y), (x, y - 1), (x, y + 1))

    hops = nz // 2 if nx == 8 else 0
    ends = ((4, 3), (3, 4))
    via = (0, nx - 1)

    def a_copy(z):
        return pltpu.make_async_copy(a_hbm.at[0, 0, z], a_v.at[z], a_sem.at[z])

    t_in = pltpu.make_async_copy(t_hbm, t_own, in_sem.at[0])
    colour_in = pltpu.make_async_copy(colour_hbm, colour, in_sem.at[1])
    pattern_in = pltpu.make_async_copy(pattern_hbm, pattern, in_sem.at[2])
    colour_in.start()
    pattern_in.start()
    t_in.start()
    for z in range(nz):
        a_copy(z).start()

    barrier = pltpu.get_barrier_semaphore()
    for d in range(4):
        @pl.when(has_dst[d])
        def _():
            pl.semaphore_signal(
                barrier, inc=1, device_id=peers[d], device_id_type=pl.DeviceIdType.MESH
            )
    count = sum(h.astype(jnp.int32) for h in has_dst)
    if hops:
        for mine, others in ((ends[0], via), (via, ends[0])):
            here = (x == mine[0]) | (x == mine[1])
            @pl.when(here)
            def _():
                for other in others:
                    pl.semaphore_signal(
                        barrier, inc=1, device_id=(other, y),
                        device_id_type=pl.DeviceIdType.MESH,
                    )
            count = count + 2 * here.astype(jnp.int32)
    pl.semaphore_wait(barrier, count)

    def t_copy(d):
        return pltpu.make_async_remote_copy(
            src_ref=t_hbm.at[0, 0], dst_ref=th.at[d],
            send_sem=th_send.at[d], recv_sem=th_recv.at[d],
            device_id=peers[d], device_id_type=pl.DeviceIdType.MESH,
        )

    def p_copy(d, z):
        return pltpu.make_async_remote_copy(
            src_ref=sbuf.at[d, z], dst_ref=rbuf.at[d, z],
            send_sem=p_send.at[d, z], recv_sem=p_recv.at[d, z],
            device_id=peers[d], device_id_type=pl.DeviceIdType.MESH,
        )

    def hop_copy(d, z):
        return pltpu.make_async_remote_copy(
            src_ref=sbuf.at[d, z], dst_ref=hop.at[z],
            send_sem=h_send.at[z], recv_sem=h_recv.at[z],
            device_id=(via[d], y), device_id_type=pl.DeviceIdType.MESH,
        )

    def forward(d, z):
        return pltpu.make_async_remote_copy(
            src_ref=hop.at[z], dst_ref=rbuf.at[d, z],
            send_sem=f_send.at[z], recv_sem=p_recv.at[d, z],
            device_id=(ends[d][1], y), device_id_type=pl.DeviceIdType.MESH,
        )

    def send(d, z, do):
        by_hop = False
        if hops and d < 2:
            by_hop = (x == ends[d][0]) & (z < hops)

            @pl.when(by_hop)
            def _():
                do(hop_copy(d, jnp.minimum(z, hops - 1)))

        @pl.when(jnp.logical_and(has_dst[d], jnp.logical_not(by_hop)))
        def _():
            do(p_copy(d, z))

    for d in (2, 3, 0, 1):
        @pl.when(has_dst[d])
        def _():
            t_copy(d).start()

    for d in range(4):
        @pl.when(jnp.logical_not(has_src[d]))
        def _():
            th[d] = jnp.zeros(th.shape[1:], BF)
            rbuf[d] = jnp.zeros(rbuf.shape[1:], BF)

    def bit(value, shift):
        return ((value >> shift) & 1).astype(F32)

    def p_of(i):
        return bit(colour[0, 0, jnp.clip(i, 0, nx - 1)], 2)

    def q_of(j):
        return bit(colour[jnp.clip(j, 0, ny - 1), 0, 0], 1)

    def r_of(z):
        return bit(colour[0, z, 0], 0)

    def hits(value):
        return (1.0 - value, value)

    def times(tile, scalar):
        return tile * jnp.full(tile.shape, scalar, F32).astype(BF)

    def place(dst, which, high, source):
        zero = jnp.zeros((blk, 4 * blk), BF)
        dst[which, 0:blk, :] = zero
        dst[which, (nz + 1) * blk : (nz + 2) * blk, :] = zero

        def step(z, carry):
            tile = source(z)
            rows = pl.ds(pl.multiple_of((z + 1) * blk, blk), blk)
            r = r_of(z)
            for h in range(2):
                for l in range(2):
                    dst[which, rows, pl.ds((2 * h + l) * blk, blk)] = times(
                        tile, hits(high)[h] * hits(r)[l]
                    )
            return carry

        lax.fori_loop(0, nz, step, 0)

    colour_in.wait()
    t_in.wait()
    place(td, 1, p_of(x), lambda z: t_own[0, 0, z])
    place(tt, 1, q_of(y), lambda z: t_own[0, 0, z])

    pattern_in.wait()

    def mask_step(z, carry):
        a_copy(z).wait()
        for o in range(27):
            a_v[z, o] = times(a_v[z, o], pattern[0, 0, z, o].astype(F32))
        return carry

    lax.fori_loop(0, nz, mask_step, 0)

    def take(d, dst, which, high):
        @pl.when(has_src[d])
        def _():
            t_copy(d).wait_recv()
        place(dst, which, high, lambda z: th[d, z])

    def direct(z, y_steps):
        rows = pl.ds(pl.multiple_of(z * blk, blk), 3 * blk)
        right = jnp.concatenate([td[i, rows, :] for i in range(3)], axis=0)
        left = jnp.concatenate(
            [
                jnp.concatenate(
                    [a_v[z, i * 9 + (dy + 1) * 3 + k] for i in range(3) for k in range(3)], axis=1
                )
                for dy in y_steps
            ],
            axis=0,
        )
        return jnp.dot(left, right, preferred_element_type=F32)

    def transposed(z, x_steps):
        rows = pl.ds(pl.multiple_of(z * blk, blk), 3 * blk)
        right = jnp.concatenate([tt[j, rows, :] for j in range(3)], axis=0)
        left = jnp.concatenate(
            [
                jnp.concatenate(
                    [
                        a_v[jnp.clip(z - 1 + e, 0, nz - 1), (dx + 1) * 9 + (2 - j) * 3 + 2 - e]
                        for dx in x_steps
                    ],
                    axis=1,
                )
                for j in range(3)
                for e in range(3)
            ],
            axis=0,
        )
        return lax.dot_general(
            left, right, (((0,), (0,)), ((), ())), preferred_element_type=F32
        )

    def edge(product, steps, first):
        def step(z, carry):
            part = product(z, steps).astype(BF)
            for k in range(2):
                d = first + k
                sbuf[d, z] = part[k * blk : (k + 1) * blk]
                send(d, z, lambda copy: copy.start())
            return carry

        lax.fori_loop(0, nz, step, 0)

    take(0, td, 2, p_of(x + 1))
    take(1, td, 0, p_of(x - 1))
    edge(direct, (1, -1), 2)
    take(2, tt, 2, q_of(y + 1))
    take(3, tt, 0, q_of(y - 1))
    edge(transposed, (-1, 1), 0)

    def own_step(z, carry):
        own[0, z] = direct(z, (0,))
        own[1, z] = transposed(z, (0,))
        return carry

    lax.fori_loop(0, nz, own_step, 0)

    for d in range(2):
        if hops:
            @pl.when(x == via[d])
            def _():
                for z in range(hops):
                    hop_copy(d, z).wait_recv()
                    forward(d, z).start()

    px, qy = p_of(x), q_of(y)
    diagonal = lax.broadcasted_iota(jnp.int32, (blk, blk), 0) == lax.broadcasted_iota(
        jnp.int32, (blk, blk), 1
    )

    def final_step(z, carry):
        centre = jnp.where(diagonal, a_v[z, 13].astype(F32), 0.0)
        scale = OMEGA / jnp.sum(centre, axis=1, keepdims=True)
        tile = t_own[0, 0, z].astype(F32)
        r = r_of(z)
        for which in (1, 0):
            first = 2 if which == 0 else 0
            for d in (first, first + 1):
                @pl.when(has_src[d])
                def _():
                    p_copy(d, z).wait_recv()
            here, above, below = (
                (qy, q_of(y + 1), q_of(y - 1)) if which == 0 else (px, p_of(x + 1), p_of(x - 1))
            )
            for h in range(2):
                for l in range(2):
                    columns = pl.ds((2 * h + l) * blk, blk)
                    mine = own[which, z, :, columns] * scale
                    up = rbuf[first, z, :, columns].astype(F32) * scale
                    down = rbuf[first + 1, z, :, columns].astype(F32) * scale
                    for v in range(2):
                        total = (
                            mine * hits(here)[v] + up * hits(above)[v] + down * hits(below)[v]
                        )
                        p, q = (h, v) if which == 0 else (v, h)
                        keep = hits(px)[p] * hits(qy)[q] * hits(r)[l]
                        (pro, res)[which][0, 0, z, 4 * p + 2 * q + l] = (tile * keep - total).astype(BF)
        return carry

    lax.fori_loop(0, nz, final_step, 0)

    for z in range(nz):
        for d in range(4):
            send(d, z, lambda copy: copy.wait_send())
    for d in range(2):
        if hops:
            @pl.when(x == via[d])
            def _():
                for z in range(hops):
                    forward(d, z).wait_send()
    for d in range(4):
        @pl.when(has_dst[d])
        def _():
            t_copy(d).wait_send()


def store_kernel(pro, res, pro_hbm, res_hbm, sem):
    nz = pro.shape[2]
    copies = [
        pltpu.make_async_copy(src.at[0, 0, z], dst.at[0, 0, z], sem.at[i, z])
        for i, (src, dst) in enumerate(((pro, pro_hbm), (res, res_hbm)))
        for z in range(nz)
    ]
    for copy in copies:
        copy.start()
    for copy in copies:
        copy.wait()


def body(nx, ny, a_tiles, pattern, t_tiles, colour):
    nz, blk = a_tiles.shape[2], a_tiles.shape[-1]
    colour = jnp.transpose(colour, (1, 2, 0))
    out = jax.ShapeDtypeStruct((1, 1, nz, SLOTS, blk, blk), BF)
    hbm = pl.BlockSpec(memory_space=pltpu.HBM)
    vmem = pl.BlockSpec(memory_space=pltpu.VMEM)
    pro, res = pl.pallas_call(
        functools.partial(kernel, nx, ny, nz, blk),
        out_shape=(out, out),
        in_specs=[hbm] * 4,
        out_specs=(vmem, vmem),
        scratch_shapes=[
            pltpu.SMEM(pattern.shape, jnp.int32),
            pltpu.SMEM(colour.shape, jnp.int32),
            pltpu.VMEM(t_tiles.shape, BF),
            pltpu.VMEM((nz, 27, blk, blk), BF),
            pltpu.VMEM((4, nz, blk, blk), BF),
            pltpu.VMEM((3, (nz + 2) * blk, 4 * blk), BF),
            pltpu.VMEM((3, (nz + 2) * blk, 4 * blk), BF),
            pltpu.VMEM((4, nz, blk, 4 * blk), BF),
            pltpu.VMEM((4, nz, blk, 4 * blk), BF),
            pltpu.VMEM((2, nz, blk, 4 * blk), F32),
            pltpu.VMEM((nz // 2, blk, 4 * blk), BF),
            pltpu.SemaphoreType.DMA((3,)),
            pltpu.SemaphoreType.DMA((nz,)),
            pltpu.SemaphoreType.DMA((4,)),
            pltpu.SemaphoreType.DMA((4,)),
            pltpu.SemaphoreType.DMA((4, nz)),
            pltpu.SemaphoreType.DMA((4, nz)),
            pltpu.SemaphoreType.DMA((nz // 2,)),
            pltpu.SemaphoreType.DMA((nz // 2,)),
            pltpu.SemaphoreType.DMA((nz // 2,)),
        ],
        compiler_params=pltpu.CompilerParams(
            collective_id=0, has_side_effects=True, vmem_limit_bytes=28 * 1024 * 1024
        ),
        cost_estimate=pl.CostEstimate(
            flops=3_600_000_000, bytes_accessed=6_000_000, transcendentals=0
        ),
    )(*(pltpu.with_memory_space_constraint(v, pltpu.HBM) for v in (pattern, colour, a_tiles, t_tiles)))
    return pl.pallas_call(
        store_kernel,
        out_shape=(out, out),
        in_specs=[vmem, vmem],
        out_specs=(hbm, hbm),
        scratch_shapes=[pltpu.SemaphoreType.DMA((2, nz))],compiler_params=pltpu.CompilerParams(vmem_limit_bytes=2*1024*1024),
    )(pro, res)


def solution(mesh):
    in_specs = (
        P("row", "col", None, None, None, None),
        P("row", "col", None, None),
        P("row", "col", None, None, None),
        P(),
    )
    out_specs = (P("row", "col", None, None, None, None), P("row", "col", None, None, None, None))
    fn = functools.partial(body, mesh.shape["row"], mesh.shape["col"])
    return jax.shard_map(fn, mesh=mesh, in_specs=in_specs, out_specs=out_specs, check_vma=False)
```

```python
import functools

import jax
import jax.numpy as jnp
from jax import lax
from jax.experimental import pallas as pl
from jax.experimental.pallas import tpu as pltpu
from jax.sharding import PartitionSpec as P

SLOTS = 8
OMEGA = 2.0 / 3.0
BF = jnp.bfloat16
F32 = jnp.float32


def kernel(
    nx, ny, nz, blk,
    pattern_hbm, colour_hbm, a_hbm, t_hbm, pro, res,
    pattern, colour, t_own, a_v, th, td, tt, sbuf, rbuf, own, hop,
    in_sem, a_sem, th_send, th_recv, p_send, p_recv, h_send, h_recv, f_send,
):
    x = lax.axis_index("row")
    y = lax.axis_index("col")
    has_dst = (x > 0, x < nx - 1, y > 0, y < ny - 1)
    has_src = (x < nx - 1, x > 0, y < ny - 1, y > 0)
    peers = ((x - 1, y), (x + 1, y), (x, y - 1), (x, y + 1))

    hops = nz // 2 if nx == 8 else 0
    ends = ((4, 3), (3, 4))
    via = (0, nx - 1)

    def a_copy(z):
        return pltpu.make_async_copy(a_hbm.at[0, 0, z], a_v.at[z], a_sem.at[z])

    t_in = pltpu.make_async_copy(t_hbm, t_own, in_sem.at[0])
    colour_in = pltpu.make_async_copy(colour_hbm, colour, in_sem.at[1])
    pattern_in = pltpu.make_async_copy(pattern_hbm, pattern, in_sem.at[2])
    colour_in.start()
    pattern_in.start()
    t_in.start()
    for z in range(nz):
        a_copy(z).start()

    barrier = pltpu.get_barrier_semaphore()
    for d in range(4):
        @pl.when(has_dst[d])
        def _():
            pl.semaphore_signal(
                barrier, inc=1, device_id=peers[d], device_id_type=pl.DeviceIdType.MESH
            )
    count = sum(h.astype(jnp.int32) for h in has_dst)
    if hops:
        for mine, others in ((ends[0], via), (via, ends[0])):
            here = (x == mine[0]) | (x == mine[1])
            @pl.when(here)
            def _():
                for other in others:
                    pl.semaphore_signal(
                        barrier, inc=1, device_id=(other, y),
                        device_id_type=pl.DeviceIdType.MESH,
                    )
            count = count + 2 * here.astype(jnp.int32)
    pl.semaphore_wait(barrier, count)

    def t_copy(d):
        return pltpu.make_async_remote_copy(
            src_ref=t_hbm.at[0, 0], dst_ref=th.at[d],
            send_sem=th_send.at[d], recv_sem=th_recv.at[d],
            device_id=peers[d], device_id_type=pl.DeviceIdType.MESH,
        )

    def p_copy(d, z):
        return pltpu.make_async_remote_copy(
            src_ref=sbuf.at[d, z], dst_ref=rbuf.at[d, z],
            send_sem=p_send.at[d, z], recv_sem=p_recv.at[d, z],
            device_id=peers[d], device_id_type=pl.DeviceIdType.MESH,
        )

    def hop_copy(d, z):
        return pltpu.make_async_remote_copy(
            src_ref=sbuf.at[d, z], dst_ref=hop.at[z],
            send_sem=h_send.at[z], recv_sem=h_recv.at[z],
            device_id=(via[d], y), device_id_type=pl.DeviceIdType.MESH,
        )

    def forward(d, z):
        return pltpu.make_async_remote_copy(
            src_ref=hop.at[z], dst_ref=rbuf.at[d, z],
            send_sem=f_send.at[z], recv_sem=p_recv.at[d, z],
            device_id=(ends[d][1], y), device_id_type=pl.DeviceIdType.MESH,
        )

    def send(d, z, do):
        by_hop = False
        if hops and d < 2:
            by_hop = (x == ends[d][0]) & (z < hops)

            @pl.when(by_hop)
            def _():
                do(hop_copy(d, jnp.minimum(z, hops - 1)))

        @pl.when(jnp.logical_and(has_dst[d], jnp.logical_not(by_hop)))
        def _():
            do(p_copy(d, z))

    for d in (2, 3, 0, 1):
        @pl.when(has_dst[d])
        def _():
            t_copy(d).start()

    for d in range(4):
        @pl.when(jnp.logical_not(has_src[d]))
        def _():
            th[d] = jnp.zeros(th.shape[1:], BF)
            rbuf[d] = jnp.zeros(rbuf.shape[1:], BF)

    def bit(value, shift):
        return ((value >> shift) & 1).astype(F32)

    def p_of(i):
        return bit(colour[0, 0, jnp.clip(i, 0, nx - 1)], 2)

    def q_of(j):
        return bit(colour[jnp.clip(j, 0, ny - 1), 0, 0], 1)

    def r_of(z):
        return bit(colour[0, z, 0], 0)

    def hits(value):
        return (1.0 - value, value)

    def times(tile, scalar):
        return tile * jnp.full(tile.shape, scalar, F32).astype(BF)

    def place(dst, which, high, source):
        zero = jnp.zeros((blk, 4 * blk), BF)
        dst[which, 0:blk, :] = zero
        dst[which, (nz + 1) * blk : (nz + 2) * blk, :] = zero

        def step(z, carry):
            tile = source(z)
            rows = pl.ds(pl.multiple_of((z + 1) * blk, blk), blk)
            r = r_of(z)
            for h in range(2):
                for l in range(2):
                    dst[which, rows, pl.ds((2 * h + l) * blk, blk)] = times(
                        tile, hits(high)[h] * hits(r)[l]
                    )
            return carry

        lax.fori_loop(0, nz, step, 0)

    colour_in.wait()
    t_in.wait()
    place(td, 1, p_of(x), lambda z: t_own[0, 0, z])
    place(tt, 1, q_of(y), lambda z: t_own[0, 0, z])

    pattern_in.wait()

    def mask_step(z, carry):
        a_copy(z).wait()
        for o in range(27):
            a_v[z, o] = times(a_v[z, o], pattern[0, 0, z, o].astype(F32))
        return carry

    lax.fori_loop(0, nz, mask_step, 0)

    def take(d, dst, which, high):
        @pl.when(has_src[d])
        def _():
            t_copy(d).wait_recv()
        place(dst, which, high, lambda z: th[d, z])

    def direct(z, y_steps):
        rows = pl.ds(pl.multiple_of(z * blk, blk), 3 * blk)
        right = jnp.concatenate([td[i, rows, :] for i in range(3)], axis=0)
        left = jnp.concatenate(
            [
                jnp.concatenate(
                    [a_v[z, i * 9 + (dy + 1) * 3 + k] for i in range(3) for k in range(3)], axis=1
                )
                for dy in y_steps
            ],
            axis=0,
        )
        return jnp.dot(left, right, preferred_element_type=F32)

    def transposed(z, x_steps):
        rows = pl.ds(pl.multiple_of(z * blk, blk), 3 * blk)
        right = jnp.concatenate([tt[j, rows, :] for j in range(3)], axis=0)
        left = jnp.concatenate(
            [
                jnp.concatenate(
                    [
                        a_v[jnp.clip(z - 1 + e, 0, nz - 1), (dx + 1) * 9 + (2 - j) * 3 + 2 - e]
                        for dx in x_steps
                    ],
                    axis=1,
                )
                for j in range(3)
                for e in range(3)
            ],
            axis=0,
        )
        return lax.dot_general(
            left, right, (((0,), (0,)), ((), ())), preferred_element_type=F32
        )

    def edge(product, steps, first, low, high):
        def step(z, carry):
            part = product(z, steps).astype(BF)
            for k in range(2):
                d = first + k
                sbuf[d, z] = part[k * blk : (k + 1) * blk]
                send(d, z, lambda copy: copy.start())
            return carry

        lax.fori_loop(low, high, step, 0)

    take(0, td, 2, p_of(x + 1))
    take(1, td, 0, p_of(x - 1))
    edge(direct, (1, -1), 2, 0, nz // 2)
    take(2, tt, 2, q_of(y + 1))
    take(3, tt, 0, q_of(y - 1))
    edge(transposed, (-1, 1), 0, 0, nz // 2)
    edge(direct, (1, -1), 2, nz // 2, nz)
    edge(transposed, (-1, 1), 0, nz // 2, nz)

    def own_step(z, carry):
        own[0, z] = direct(z, (0,))
        own[1, z] = transposed(z, (0,))
        return carry

    lax.fori_loop(0, nz, own_step, 0)

    for d in range(2):
        if hops:
            @pl.when(x == via[d])
            def _():
                for z in range(hops):
                    hop_copy(d, z).wait_recv()
                    forward(d, z).start()

    px, qy = p_of(x), q_of(y)
    diagonal = lax.broadcasted_iota(jnp.int32, (blk, blk), 0) == lax.broadcasted_iota(
        jnp.int32, (blk, blk), 1
    )

    def final_step(z, carry):
        centre = jnp.where(diagonal, a_v[z, 13].astype(F32), 0.0)
        scale = OMEGA / jnp.sum(centre, axis=1, keepdims=True)
        tile = t_own[0, 0, z].astype(F32)
        r = r_of(z)
        for which in (1, 0):
            first = 2 if which == 0 else 0
            for d in (first, first + 1):
                @pl.when(has_src[d])
                def _():
                    p_copy(d, z).wait_recv()
            here, above, below = (
                (qy, q_of(y + 1), q_of(y - 1)) if which == 0 else (px, p_of(x + 1), p_of(x - 1))
            )
            for h in range(2):
                for l in range(2):
                    columns = pl.ds((2 * h + l) * blk, blk)
                    mine = own[which, z, :, columns] * scale
                    up = rbuf[first, z, :, columns].astype(F32) * scale
                    down = rbuf[first + 1, z, :, columns].astype(F32) * scale
                    for v in range(2):
                        total = (
                            mine * hits(here)[v] + up * hits(above)[v] + down * hits(below)[v]
                        )
                        p, q = (h, v) if which == 0 else (v, h)
                        keep = hits(px)[p] * hits(qy)[q] * hits(r)[l]
                        (pro, res)[which][0, 0, z, 4 * p + 2 * q + l] = (tile * keep - total).astype(BF)
        return carry

    lax.fori_loop(0, nz, final_step, 0)

    for z in range(nz):
        for d in range(4):
            send(d, z, lambda copy: copy.wait_send())
    for d in range(2):
        if hops:
            @pl.when(x == via[d])
            def _():
                for z in range(hops):
                    forward(d, z).wait_send()
    for d in range(4):
        @pl.when(has_dst[d])
        def _():
            t_copy(d).wait_send()


def store_kernel(pro, res, pro_hbm, res_hbm, sem):
    nz = pro.shape[2]
    copies = [
        pltpu.make_async_copy(src.at[0, 0, z], dst.at[0, 0, z], sem.at[i, z])
        for i, (src, dst) in enumerate(((pro, pro_hbm), (res, res_hbm)))
        for z in range(nz)
    ]
    for copy in copies:
        copy.start()
    for copy in copies:
        copy.wait()


def body(nx, ny, a_tiles, pattern, t_tiles, colour):
    nz, blk = a_tiles.shape[2], a_tiles.shape[-1]
    colour = jnp.transpose(colour, (1, 2, 0))
    out = jax.ShapeDtypeStruct((1, 1, nz, SLOTS, blk, blk), BF)
    hbm = pl.BlockSpec(memory_space=pltpu.HBM)
    vmem = pl.BlockSpec(memory_space=pltpu.VMEM)
    pro, res = pl.pallas_call(
        functools.partial(kernel, nx, ny, nz, blk),
        out_shape=(out, out),
        in_specs=[hbm] * 4,
        out_specs=(vmem, vmem),
        scratch_shapes=[
            pltpu.SMEM(pattern.shape, jnp.int32),
            pltpu.SMEM(colour.shape, jnp.int32),
            pltpu.VMEM(t_tiles.shape, BF),
            pltpu.VMEM((nz, 27, blk, blk), BF),
            pltpu.VMEM((4, nz, blk, blk), BF),
            pltpu.VMEM((3, (nz + 2) * blk, 4 * blk), BF),
            pltpu.VMEM((3, (nz + 2) * blk, 4 * blk), BF),
            pltpu.VMEM((4, nz, blk, 4 * blk), BF),
            pltpu.VMEM((4, nz, blk, 4 * blk), BF),
            pltpu.VMEM((2, nz, blk, 4 * blk), F32),
            pltpu.VMEM((nz // 2, blk, 4 * blk), BF),
            pltpu.SemaphoreType.DMA((3,)),
            pltpu.SemaphoreType.DMA((nz,)),
            pltpu.SemaphoreType.DMA((4,)),
            pltpu.SemaphoreType.DMA((4,)),
            pltpu.SemaphoreType.DMA((4, nz)),
            pltpu.SemaphoreType.DMA((4, nz)),
            pltpu.SemaphoreType.DMA((nz // 2,)),
            pltpu.SemaphoreType.DMA((nz // 2,)),
            pltpu.SemaphoreType.DMA((nz // 2,)),
        ],
        compiler_params=pltpu.CompilerParams(
            collective_id=0, has_side_effects=True, vmem_limit_bytes=28 * 1024 * 1024
        ),
        cost_estimate=pl.CostEstimate(
            flops=3_600_000_000, bytes_accessed=6_000_000, transcendentals=0
        ),
    )(*(pltpu.with_memory_space_constraint(v, pltpu.HBM) for v in (pattern, colour, a_tiles, t_tiles)))
    return pl.pallas_call(
        store_kernel,
        out_shape=(out, out),
        in_specs=[vmem, vmem],
        out_specs=(hbm, hbm),
        scratch_shapes=[pltpu.SemaphoreType.DMA((2, nz))],compiler_params=pltpu.CompilerParams(vmem_limit_bytes=2*1024*1024),
    )(pro, res)


def solution(mesh):
    in_specs = (
        P("row", "col", None, None, None, None),
        P("row", "col", None, None),
        P("row", "col", None, None, None),
        P(),
    )
    out_specs = (P("row", "col", None, None, None, None), P("row", "col", None, None, None, None))
    fn = functools.partial(body, mesh.shape["row"], mesh.shape["col"])
    return jax.shard_map(fn, mesh=mesh, in_specs=in_specs, out_specs=out_specs, check_vma=False)
```

```python
import functools

import jax
import jax.numpy as jnp
from jax import lax
from jax.experimental import pallas as pl
from jax.experimental.pallas import tpu as pltpu
from jax.sharding import PartitionSpec as P

SLOTS = 8
OMEGA = 2.0 / 3.0
BF = jnp.bfloat16
F32 = jnp.float32


def kernel(
    nx, ny, nz, blk,
    pattern_hbm, colour_hbm, a_hbm, t_hbm, pro, res,
    pattern, colour, t_own, a_v, th, td, tt, sbuf, rbuf, own, hop,
    in_sem, a_sem, th_send, th_recv, p_send, p_recv, h_send, h_recv, f_send,
):
    x = lax.axis_index("row")
    y = lax.axis_index("col")
    has_dst = (x > 0, x < nx - 1, y > 0, y < ny - 1)
    has_src = (x < nx - 1, x > 0, y < ny - 1, y > 0)
    peers = ((x - 1, y), (x + 1, y), (x, y - 1), (x, y + 1))

    hops = nz // 2 if nx == 8 else 0
    ends = ((4, 3), (3, 4))
    via = (0, nx - 1)

    def a_copy(z):
        return pltpu.make_async_copy(a_hbm.at[0, 0, z], a_v.at[z], a_sem.at[z])

    t_in = pltpu.make_async_copy(t_hbm, t_own, in_sem.at[0])
    colour_in = pltpu.make_async_copy(colour_hbm, colour, in_sem.at[1])
    pattern_in = pltpu.make_async_copy(pattern_hbm, pattern, in_sem.at[2])
    colour_in.start()
    pattern_in.start()
    t_in.start()
    for z in range(nz):
        a_copy(z).start()

    barrier = pltpu.get_barrier_semaphore()
    for d in range(4):
        @pl.when(has_dst[d])
        def _():
            pl.semaphore_signal(
                barrier, inc=1, device_id=peers[d], device_id_type=pl.DeviceIdType.MESH
            )
    count = sum(h.astype(jnp.int32) for h in has_dst)
    if hops:
        for mine, others in ((ends[0], via), (via, ends[0])):
            here = (x == mine[0]) | (x == mine[1])
            @pl.when(here)
            def _():
                for other in others:
                    pl.semaphore_signal(
                        barrier, inc=1, device_id=(other, y),
                        device_id_type=pl.DeviceIdType.MESH,
                    )
            count = count + 2 * here.astype(jnp.int32)
    pl.semaphore_wait(barrier, count)

    def t_copy(d):
        return pltpu.make_async_remote_copy(
            src_ref=t_hbm.at[0, 0], dst_ref=th.at[d],
            send_sem=th_send.at[d], recv_sem=th_recv.at[d],
            device_id=peers[d], device_id_type=pl.DeviceIdType.MESH,
        )

    def p_copy(d, z):
        return pltpu.make_async_remote_copy(
            src_ref=sbuf.at[d, z], dst_ref=rbuf.at[d, z],
            send_sem=p_send.at[d, z], recv_sem=p_recv.at[d, z],
            device_id=peers[d], device_id_type=pl.DeviceIdType.MESH,
        )

    def hop_copy(d, z):
        return pltpu.make_async_remote_copy(
            src_ref=sbuf.at[d, z], dst_ref=hop.at[z],
            send_sem=h_send.at[z], recv_sem=h_recv.at[z],
            device_id=(via[d], y), device_id_type=pl.DeviceIdType.MESH,
        )

    def forward(d, z):
        return pltpu.make_async_remote_copy(
            src_ref=hop.at[z], dst_ref=rbuf.at[d, z],
            send_sem=f_send.at[z], recv_sem=p_recv.at[d, z],
            device_id=(ends[d][1], y), device_id_type=pl.DeviceIdType.MESH,
        )

    def send(d, z, do):
        by_hop = False
        if hops and d < 2:
            by_hop = (x == ends[d][0]) & (z < hops)

            @pl.when(by_hop)
            def _():
                do(hop_copy(d, jnp.minimum(z, hops - 1)))

        @pl.when(jnp.logical_and(has_dst[d], jnp.logical_not(by_hop)))
        def _():
            do(p_copy(d, z))

    for d in (0, 1, 2, 3):
        @pl.when(has_dst[d])
        def _():
            t_copy(d).start()

    for d in range(4):
        @pl.when(jnp.logical_not(has_src[d]))
        def _():
            th[d] = jnp.zeros(th.shape[1:], BF)
            rbuf[d] = jnp.zeros(rbuf.shape[1:], BF)

    def bit(value, shift):
        return ((value >> shift) & 1).astype(F32)

    def p_of(i):
        return bit(colour[0, 0, jnp.clip(i, 0, nx - 1)], 2)

    def q_of(j):
        return bit(colour[jnp.clip(j, 0, ny - 1), 0, 0], 1)

    def r_of(z):
        return bit(colour[0, z, 0], 0)

    def hits(value):
        return (1.0 - value, value)

    def times(tile, scalar):
        return tile * jnp.full(tile.shape, scalar, F32).astype(BF)

    def place(dst, which, high, source):
        zero = jnp.zeros((blk, 4 * blk), BF)
        dst[which, 0:blk, :] = zero
        dst[which, (nz + 1) * blk : (nz + 2) * blk, :] = zero

        def step(z, carry):
            tile = source(z)
            rows = pl.ds(pl.multiple_of((z + 1) * blk, blk), blk)
            r = r_of(z)
            for h in range(2):
                for l in range(2):
                    dst[which, rows, pl.ds((2 * h + l) * blk, blk)] = times(
                        tile, hits(high)[h] * hits(r)[l]
                    )
            return carry

        lax.fori_loop(0, nz, step, 0)

    colour_in.wait()
    t_in.wait()
    place(td, 1, p_of(x), lambda z: t_own[0, 0, z])
    place(tt, 1, q_of(y), lambda z: t_own[0, 0, z])

    pattern_in.wait()

    def mask_step(z, carry):
        a_copy(z).wait()
        for o in range(27):
            a_v[z, o] = times(a_v[z, o], pattern[0, 0, z, o].astype(F32))
        return carry

    lax.fori_loop(0, nz, mask_step, 0)

    def take(d, dst, which, high):
        @pl.when(has_src[d])
        def _():
            t_copy(d).wait_recv()
        place(dst, which, high, lambda z: th[d, z])

    def direct(z, y_steps):
        rows = pl.ds(pl.multiple_of(z * blk, blk), 3 * blk)
        right = jnp.concatenate([td[i, rows, :] for i in range(3)], axis=0)
        left = jnp.concatenate(
            [
                jnp.concatenate(
                    [a_v[z, i * 9 + (dy + 1) * 3 + k] for i in range(3) for k in range(3)], axis=1
                )
                for dy in y_steps
            ],
            axis=0,
        )
        return jnp.dot(left, right, preferred_element_type=F32)

    def transposed(z, x_steps):
        rows = pl.ds(pl.multiple_of(z * blk, blk), 3 * blk)
        right = jnp.concatenate([tt[j, rows, :] for j in range(3)], axis=0)
        left = jnp.concatenate(
            [
                jnp.concatenate(
                    [
                        a_v[jnp.clip(z - 1 + e, 0, nz - 1), (dx + 1) * 9 + (2 - j) * 3 + 2 - e]
                        for dx in x_steps
                    ],
                    axis=1,
                )
                for j in range(3)
                for e in range(3)
            ],
            axis=0,
        )
        return lax.dot_general(
            left, right, (((0,), (0,)), ((), ())), preferred_element_type=F32
        )

    def edge(product, steps, first, low, high):
        def step(z, carry):
            part = product(z, steps).astype(BF)
            for k in range(2):
                d = first + k
                sbuf[d, z] = part[k * blk : (k + 1) * blk]
                send(d, z, lambda copy: copy.start())
            return carry

        lax.fori_loop(low, high, step, 0)

    take(0, td, 2, p_of(x + 1))
    take(1, td, 0, p_of(x - 1))
    edge(direct, (1, -1), 2, 0, nz // 2)
    take(2, tt, 2, q_of(y + 1))
    take(3, tt, 0, q_of(y - 1))
    edge(transposed, (-1, 1), 0, 0, nz // 2)
    edge(direct, (1, -1), 2, nz // 2, nz)
    edge(transposed, (-1, 1), 0, nz // 2, nz)

    def own_step(z, carry):
        own[0, z] = direct(z, (0,))
        own[1, z] = transposed(z, (0,))
        return carry

    lax.fori_loop(0, nz, own_step, 0)

    for d in range(2):
        if hops:
            @pl.when(x == via[d])
            def _():
                for z in range(hops):
                    hop_copy(d, z).wait_recv()
                    forward(d, z).start()

    px, qy = p_of(x), q_of(y)
    diagonal = lax.broadcasted_iota(jnp.int32, (blk, blk), 0) == lax.broadcasted_iota(
        jnp.int32, (blk, blk), 1
    )

    def final_step(z, carry):
        centre = jnp.where(diagonal, a_v[z, 13].astype(F32), 0.0)
        scale = OMEGA / jnp.sum(centre, axis=1, keepdims=True)
        tile = t_own[0, 0, z].astype(F32)
        r = r_of(z)
        for which in (1, 0):
            first = 2 if which == 0 else 0
            for d in (first, first + 1):
                @pl.when(has_src[d])
                def _():
                    p_copy(d, z).wait_recv()
            here, above, below = (
                (qy, q_of(y + 1), q_of(y - 1)) if which == 0 else (px, p_of(x + 1), p_of(x - 1))
            )
            for h in range(2):
                for l in range(2):
                    columns = pl.ds((2 * h + l) * blk, blk)
                    mine = own[which, z, :, columns] * scale
                    up = rbuf[first, z, :, columns].astype(F32) * scale
                    down = rbuf[first + 1, z, :, columns].astype(F32) * scale
                    for v in range(2):
                        total = (
                            mine * hits(here)[v] + up * hits(above)[v] + down * hits(below)[v]
                        )
                        p, q = (h, v) if which == 0 else (v, h)
                        keep = hits(px)[p] * hits(qy)[q] * hits(r)[l]
                        (pro, res)[which][0, 0, z, 4 * p + 2 * q + l] = (tile * keep - total).astype(BF)
        return carry

    lax.fori_loop(0, nz, final_step, 0)

    for z in range(nz):
        for d in range(4):
            send(d, z, lambda copy: copy.wait_send())
    for d in range(2):
        if hops:
            @pl.when(x == via[d])
            def _():
                for z in range(hops):
                    forward(d, z).wait_send()
    for d in range(4):
        @pl.when(has_dst[d])
        def _():
            t_copy(d).wait_send()


def store_kernel(pro, res, pro_hbm, res_hbm, sem):
    nz = pro.shape[2]
    copies = [
        pltpu.make_async_copy(src.at[0, 0, z], dst.at[0, 0, z], sem.at[i, z])
        for i, (src, dst) in enumerate(((pro, pro_hbm), (res, res_hbm)))
        for z in range(nz)
    ]
    for copy in copies:
        copy.start()
    for copy in copies:
        copy.wait()


def body(nx, ny, a_tiles, pattern, t_tiles, colour):
    nz, blk = a_tiles.shape[2], a_tiles.shape[-1]
    colour = jnp.transpose(colour, (1, 2, 0))
    out = jax.ShapeDtypeStruct((1, 1, nz, SLOTS, blk, blk), BF)
    hbm = pl.BlockSpec(memory_space=pltpu.HBM)
    vmem = pl.BlockSpec(memory_space=pltpu.VMEM)
    pro, res = pl.pallas_call(
        functools.partial(kernel, nx, ny, nz, blk),
        out_shape=(out, out),
        in_specs=[hbm] * 4,
        out_specs=(vmem, vmem),
        scratch_shapes=[
            pltpu.SMEM(pattern.shape, jnp.int32),
            pltpu.SMEM(colour.shape, jnp.int32),
            pltpu.VMEM(t_tiles.shape, BF),
            pltpu.VMEM((nz, 27, blk, blk), BF),
            pltpu.VMEM((4, nz, blk, blk), BF),
            pltpu.VMEM((3, (nz + 2) * blk, 4 * blk), BF),
            pltpu.VMEM((3, (nz + 2) * blk, 4 * blk), BF),
            pltpu.VMEM((4, nz, blk, 4 * blk), BF),
            pltpu.VMEM((4, nz, blk, 4 * blk), BF),
            pltpu.VMEM((2, nz, blk, 4 * blk), F32),
            pltpu.VMEM((nz // 2, blk, 4 * blk), BF),
            pltpu.SemaphoreType.DMA((3,)),
            pltpu.SemaphoreType.DMA((nz,)),
            pltpu.SemaphoreType.DMA((4,)),
            pltpu.SemaphoreType.DMA((4,)),
            pltpu.SemaphoreType.DMA((4, nz)),
            pltpu.SemaphoreType.DMA((4, nz)),
            pltpu.SemaphoreType.DMA((nz // 2,)),
            pltpu.SemaphoreType.DMA((nz // 2,)),
            pltpu.SemaphoreType.DMA((nz // 2,)),
        ],
        compiler_params=pltpu.CompilerParams(
            collective_id=0, has_side_effects=True, vmem_limit_bytes=28 * 1024 * 1024
        ),
        cost_estimate=pl.CostEstimate(
            flops=3_600_000_000, bytes_accessed=6_000_000, transcendentals=0
        ),
    )(*(pltpu.with_memory_space_constraint(v, pltpu.HBM) for v in (pattern, colour, a_tiles, t_tiles)))
    return pl.pallas_call(
        store_kernel,
        out_shape=(out, out),
        in_specs=[vmem, vmem],
        out_specs=(hbm, hbm),
        scratch_shapes=[pltpu.SemaphoreType.DMA((2, nz))],compiler_params=pltpu.CompilerParams(vmem_limit_bytes=2*1024*1024),
    )(pro, res)


def solution(mesh):
    in_specs = (
        P("row", "col", None, None, None, None),
        P("row", "col", None, None),
        P("row", "col", None, None, None),
        P(),
    )
    out_specs = (P("row", "col", None, None, None, None), P("row", "col", None, None, None, None))
    fn = functools.partial(body, mesh.shape["row"], mesh.shape["col"])
    return jax.shard_map(fn, mesh=mesh, in_specs=in_specs, out_specs=out_specs, check_vma=False)
```
